256 devices in a mesh: queue: 16 (over y, x_lo, core), heads: 16 (over x_hi, z).
Axes of the slice: x: 4 (x_hi: 2, x_lo: 2; x = x_hi * 2 + x_lo), y: 4, z: 8, core: 2. Of those that a mesh axis runs over, the one named last changes fastest.
Arguments:
- latents: bfloat16 [16, 1024, 3072], P('queue', 'heads'), may hold values from -6 to 6
- t_index: int32 [16], P('queue'), may hold values from 0 to 999
- window_start: int32 [16], P('queue'), may hold values from 0 to 12, as said below
- w_mod: bfloat16 [512, 9216], P(None, 'heads'), may hold values from -0.25 to 0.25
- w_qkv: bfloat16 [3072, 9216], P(None, 'heads'), may hold values from -0.109375 to 0.109375
- q_gain: float32 [64], replicated, may hold values from 1.5 to 6
- k_gain: float32 [64], replicated, may hold values from 1.5 to 6
- w_out: bfloat16 [3072, 3072], P('heads'), may hold values from -0.109375 to 0.109375
Outputs:
- shifted: bfloat16 [16, 1024, 3072], P('queue', 'heads')
The draws below stay inside these ranges and needn't reach their ends.
Inputs may be any that keep to these rules, and one draw needn't show every extreme that they name: window_start of frame f lies between max(0, f - 3) and min(f, 12).
All inputs are finite; a program needn't handle non-finite values.
Results may differ from the reference program's by a relative error of at most 0.019.
Values may be sent and summed in bfloat16 or wider, within the bound.
No kernel may reach another device: no remote copies, remote signals or barrier semaphores. Data moves between devices by JAX's collectives and lax.ppermute only.
A program may use at most 128 MiB of HBM per device.

```python
import math
import jax
import jax.numpy as jnp
from jax import lax

D = 3072
HEADS = 48
HEAD_DIM = 64
TE = 512
WINDOW = 4
FRAMES = 16
FRAME_TOKENS = 1024


def draw_window_start(key, part):
    key = jax.random.fold_in(key, 11)
    frame = jnp.arange(FRAMES, dtype=jnp.int32)
    back = jax.random.randint(key, (FRAMES,), 0, WINDOW, dtype=jnp.int32)
    return jnp.clip(frame - back, 0, FRAMES - WINDOW).astype(jnp.int32)


def gain_values(key, low, high):
    return jax.random.uniform(key, (HEAD_DIM,), jnp.float32, low, high)


def draw_q_gain(key, part):
    key = jax.random.fold_in(key, 21)
    return gain_values(key, 1.5, 3.0)


def draw_k_gain(key, part):
    key = jax.random.fold_in(key, 31)
    return gain_values(key, 1.5, 3.0)


def with_ends(entries, own_key, least, high):
    longest = entries.shape.index(max(entries.shape))
    spots = []
    for shift in (0, 1):
        where = [jax.random.randint(jax.random.fold_in(own_key, axis), (), 0, length) for axis, length in enumerate(entries.shape)]
        where[longest] = (where[longest] + shift) % entries.shape[longest]
        spots.append(tuple(where))
    return entries.at[spots[0]].set(least).at[spots[1]].set(high)


def level_of(key, shape, split, low, top_value):
    factor_of = 1.0
    for axis_at, parts in split:
        steps = jax.random.uniform(jax.random.fold_in(jax.random.fold_in(key, 6), axis_at), (parts,), jnp.float32, low / len(split), top_value / len(split))
        factor_of = factor_of * jnp.repeat(jnp.exp(steps), shape[axis_at] // parts).reshape((-1,) + (1,) * (len(shape) - 1 - axis_at))
    return factor_of


def centred(key, extent, scale, limit, shards=(), kind=jnp.bfloat16):
    drawn = jax.random.normal(key, extent, jnp.float32) * scale
    if len(shards) > 0:
        drawn = level_of(key, extent, shards, -0.22, 0.18) * drawn
    return jnp.clip(drawn, min=-limit, max=limit).astype(kind)


def setup_inputs(seed: int = 0) -> dict:
    key_list = jax.random.split(jax.random.key(seed), 9)
    latents = centred(key_list[0], (FRAMES, FRAME_TOKENS, D), 1.0, 6.0, ((0, 16), (1, 16)))
    t_index = with_ends(jax.random.randint(key_list[1], (FRAMES,), 0, 1000), jax.random.fold_in(key_list[1], 1), 0, 999).astype(jnp.int32)
    window_start = draw_window_start(jax.random.fold_in(key_list[8], 71), 0)
    w_mod = centred(key_list[3], (TE, 3 * D), TE ** -0.5, 0.25, ((1, 16),))
    w_qkv = centred(key_list[4], (D, 3 * D), D ** -0.5, 0.109375, ((1, 16),))
    q_gain = draw_q_gain(jax.random.fold_in(key_list[8], 71), 0)
    k_gain = draw_k_gain(jax.random.fold_in(key_list[8], 71), 0)
    w_out = centred(key_list[7], (D, D), D ** -0.5, 0.109375, ((0, 16),))
    return {"latents": latents, "t_index": t_index, "window_start": window_start, "w_mod": w_mod, "w_qkv": w_qkv, "q_gain": q_gain, "k_gain": k_gain, "w_out": w_out}


def time_features(steps_float, width):
    half = width // 2
    freqs = jnp.exp(-math.log(10000.0) * jnp.arange(half, dtype=jnp.float32) / half)
    angles = steps_float[:, None] * freqs[None, :]
    return jnp.concatenate([jnp.cos(angles), jnp.sin(angles)], axis=1)

def modulate(tokens, shift, scale):
    values = tokens.astype(jnp.float32)
    center = lax.optimization_barrier(jnp.mean(values, axis=-1, keepdims=True))
    spread = lax.optimization_barrier(jnp.mean(jnp.square(values - center), axis=-1, keepdims=True))
    normal = (values - center) * lax.rsqrt(spread + 1e-05)
    return (normal * (1.0 + scale) + shift).astype(jnp.bfloat16)

def head_norm(values, gain):
    center = lax.optimization_barrier(jnp.mean(values, axis=-1, keepdims=True))
    spread = lax.optimization_barrier(jnp.mean(jnp.square(values - center), axis=-1, keepdims=True))
    return (values - center) * lax.rsqrt(spread + 1e-06) * gain

def reference(latents, t_index, window_start, w_mod, w_qkv, q_gain, k_gain, w_out):
    emb = time_features(t_index.astype(jnp.float32), TE)
    active = jax.nn.silu(emb).astype(jnp.bfloat16)
    mod = jnp.dot(active, w_mod, preferred_element_type=jnp.float32)
    shift = mod[:, None, :D]
    scale = mod[:, None, D:2 * D]
    gate = mod[:, None, 2 * D:]
    normed = modulate(latents, shift, scale)
    qkv = jnp.dot(normed.reshape(FRAMES * FRAME_TOKENS, D), w_qkv, preferred_element_type=jnp.float32)
    qkv = qkv.reshape(FRAMES, FRAME_TOKENS, HEADS, 3, HEAD_DIM)
    queries = head_norm(qkv[:, :, :, 0], q_gain).astype(jnp.bfloat16)
    keys = head_norm(qkv[:, :, :, 1], k_gain).astype(jnp.bfloat16)
    values = qkv[:, :, :, 2].astype(jnp.bfloat16)
    factor = 1.0 / math.sqrt(HEAD_DIM)

    def head_step(operands):
        query_h, key_h, value_h = operands
        scores = jnp.dot(query_h, key_h.T, preferred_element_type=jnp.float32) * factor
        top = lax.optimization_barrier(jnp.max(scores, axis=-1, keepdims=True))
        expo = jnp.exp(scores - top)
        probs = (expo / lax.optimization_barrier(jnp.sum(expo, axis=-1, keepdims=True))).astype(jnp.bfloat16)
        return jnp.dot(probs, value_h, preferred_element_type=jnp.float32).astype(jnp.bfloat16)

    def frame_step(index):
        first = window_start[index].astype(jnp.int32)
        near_keys = lax.dynamic_slice_in_dim(keys, first, WINDOW, 0).reshape(WINDOW * FRAME_TOKENS, HEADS, HEAD_DIM)
        near_values = lax.dynamic_slice_in_dim(values, first, WINDOW, 0).reshape(WINDOW * FRAME_TOKENS, HEADS, HEAD_DIM)
        own = queries[index]
        outputs = lax.map(head_step, (jnp.transpose(own, (1, 0, 2)), jnp.transpose(near_keys, (1, 0, 2)), jnp.transpose(near_values, (1, 0, 2))))
        return jnp.transpose(outputs, (1, 0, 2)).reshape(FRAME_TOKENS, D)
    attn = lax.map(frame_step, jnp.arange(FRAMES, dtype=jnp.int32))
    proj = jnp.dot(attn.reshape(FRAMES * FRAME_TOKENS, D), w_out, preferred_element_type=jnp.float32)
    proj = proj.reshape(FRAMES, FRAME_TOKENS, D)
    block = (latents.astype(jnp.float32) + gate * proj).astype(jnp.bfloat16)
    return jnp.roll(block, 1, axis=0)
```

```python
import functools
import math

import jax
import jax.numpy as jnp
from jax import lax
from jax.experimental import pallas as pl
from jax.experimental.pallas import tpu as pltpu
from jax.sharding import PartitionSpec as P

F32 = jnp.float32
BF16 = jnp.bfloat16
BOTH = ("queue", "heads")
LANES = 128
HALF = 64
RING = 8
QUEUE = 16
VMEM = pl.BlockSpec(memory_space=pltpu.VMEM)
LOG2E = 1.4426950408889634


def every_device():
    for q in range(QUEUE):
        for h in range(2 * RING):
            yield q, h


def route(move):
    pairs = []
    for q, h in every_device():
        to_q, to_ring, to_z = move(q, h // RING, h % RING)
        pairs.append((q * 2 * RING + h, (to_q % QUEUE) * 2 * RING + to_ring * RING + to_z % RING))
    return pairs


def send(value, move):
    return lax.ppermute(value, BOTH, route(move))


def along(step):
    return lambda q, ring, z: (q, ring, z + step)


def across(q, ring, z):
    return q, 1 - ring, z


def sibling(q, ring, z):
    return q ^ 1, ring, z


def ahead(step):
    return lambda q, ring, z: (q + step, ring, z)


def far(q, ring, z):
    return (q + 3 if q % 2 else q - 3), ring, z


def time_features(steps_float, width):
    half = width // 2
    freqs = jnp.exp(-math.log(10000.0) * jnp.arange(half, dtype=F32) / half)
    angles = steps_float[:, None] * freqs[None, :]
    return jnp.concatenate([jnp.cos(angles), jnp.sin(angles)], axis=1)


def gather_modulation(part):
    rows = part
    for step in (1, 2, 4):
        rows = jnp.concatenate([rows, send(rows, along(-step))], axis=0)
    other = send(rows, across)
    place = lax.axis_index("heads")
    z = place % RING
    own = lax.dynamic_slice_in_dim(jnp.concatenate([rows, rows]), (RING - z) % RING, RING, 0)
    opposite = lax.dynamic_slice_in_dim(jnp.concatenate([other, other]), (RING - z) % RING, RING, 0)
    trio = jnp.concatenate([own, opposite, own])
    return lax.dynamic_slice_in_dim(trio, (place // RING) * RING, 2 * RING, 0).reshape(1, -1)


def qkv_kernel(count, *refs):
    pieces = refs[:count]
    shift, scale, weight, q_gain, k_gain, q_out, kv_out, normed = refs[count:]
    rows = pieces[0].shape[0]
    for at, piece in enumerate(pieces):
        x = piece[...].astype(F32)
        center = jnp.mean(x, axis=-1, keepdims=True)
        x = x - center
        spread = jnp.mean(x * x, axis=-1, keepdims=True)
        x = x * lax.rsqrt(spread + 1e-05) * (1.0 + scale[...]) + shift[...]
        normed[at * rows : (at + 1) * rows, :] = x.astype(BF16)
    y = jnp.dot(normed[...], weight[...], preferred_element_type=F32)
    tokens = y.shape[0]
    low = lax.broadcasted_iota(jnp.int32, (tokens, LANES), 1) < HALF

    def halves(v):
        first = jnp.sum(jnp.where(low, v, 0.0), axis=-1, keepdims=True)
        second = jnp.sum(jnp.where(low, 0.0, v), axis=-1, keepdims=True)
        return jnp.where(low, first, second) * (1.0 / HALF)

    def norm(v, gain):
        v = v - halves(v)
        return v * lax.rsqrt(halves(v * v) + 1e-06) * gain

    q01 = norm(y[:, :LANES], q_gain[...])
    q2 = norm(y[:, LANES : 2 * LANES], q_gain[...])
    k01 = norm(y[:, 2 * LANES : 3 * LANES], k_gain[...])
    k2v1 = y[:, 3 * LANES : 4 * LANES]
    k2v1 = jnp.where(low, norm(k2v1, k_gain[...]), k2v1)
    q_out[:, :LANES] = jnp.where(low, q01, 0.0).astype(BF16)
    q_out[:, LANES : 2 * LANES] = jnp.where(low, 0.0, q01).astype(BF16)
    q_out[:, 2 * LANES :] = jnp.where(low, q2, 0.0).astype(BF16)
    kv_out[:, :LANES] = k01.astype(BF16)
    kv_out[:, LANES : 2 * LANES] = k2v1.astype(BF16)
    kv_out[:, 2 * LANES :] = y[:, 4 * LANES :].astype(BF16)


def project(pieces, shift, scale, weight, q_gain, k_gain):
    count = len(pieces)
    rows, width = pieces[0].shape
    tokens = count * rows
    shape = jax.ShapeDtypeStruct((tokens, 3 * LANES), BF16)
    return pl.pallas_call(
        functools.partial(qkv_kernel, count),
        in_specs=[VMEM] * (count + 5),
        out_specs=[VMEM] * 2,
        out_shape=[shape, shape],
        scratch_shapes=[pltpu.VMEM((tokens, width), BF16)],
        compiler_params=pltpu.CompilerParams(vmem_limit_bytes=24 * 2**20),
        cost_estimate=pl.CostEstimate(
            flops=2 * tokens * width * 640, bytes_accessed=tokens * width * 2 + width * 1280, transcendentals=0
        ),
        name="qkv",
    )(*pieces, shift, scale, weight, q_gain, k_gain)


def attend_kernel(pairs, first, last, take, q, *refs):
    frames = refs[: sum(pairs)]
    refs = refs[len(frames) :]
    if not first:
        top_in, sums_in, refs = refs[0], refs[1], refs[2:]
    if last:
        out, top, sums, held = refs
    else:
        top, sums, held = refs
    rows = q.shape[0]
    keys = frames[0].shape[0]
    if first:
        top[...] = jnp.full_like(top, -1e30)
        sums[...] = jnp.zeros_like(sums)
    else:
        top[...] = top_in[...]
        sums[...] = sums_in[...]
    at = 0
    for number, size in enumerate(pairs):
        if size == 1:
            held[number] = frames[at][...]
        else:
            one, two = frames[at], frames[at + 1]

            @pl.when(take[number] == 0)
            def _(number=number, one=one):
                held[number] = one[...]

            @pl.when(take[number] != 0)
            def _(number=number, two=two):
                held[number] = two[...]

        at += size
    block = 256
    low = lax.broadcasted_iota(jnp.int32, (keys, LANES), 1) < HALF

    @pl.loop(0, len(pairs) * (rows // block))
    def _(turn):
        number = turn // (rows // block)
        span = pl.ds(pl.multiple_of((turn % (rows // block)) * block, block), block)
        k01 = held[number, :, :LANES]
        k2v1 = held[number, :, LANES : 2 * LANES]
        v02 = held[number, :, 2 * LANES :]
        ones = jnp.ones_like(v02)
        for head, (k, v) in enumerate(
            (
                (k01, jnp.where(low, v02, ones)),
                (k01, jnp.where(low, ones, k2v1)),
                (k2v1, jnp.where(low, ones, v02)),
            )
        ):
            query = q[span, head * LANES : (head + 1) * LANES]
            s = lax.dot_general(query, k, (((1,), (1,)), ((), ())), preferred_element_type=F32)
            before = top[head, span, :]
            now = jnp.maximum(before, jnp.max(s, axis=1, keepdims=True))
            p = jnp.exp2(s - now[:, :1]).astype(BF16)
            added = jnp.dot(p, v, preferred_element_type=F32)
            sums[head, span, :] = sums[head, span, :] * jnp.exp2(before - now) + added
            top[head, span, :] = now

    if last:
        small = lax.broadcasted_iota(jnp.int32, (rows, LANES), 1) < HALF

        def whole(head):
            both = sums[head]
            return both / pltpu.roll(both, HALF, 1)

        out[:, :LANES] = jnp.where(small, whole(0), whole(1)).astype(BF16)
        out[:, LANES:] = pltpu.roll(whole(2), HALF, 1)[:, :HALF].astype(BF16)


def attend(q, groups, take, state, last):
    rows = q.shape[0]
    keys = groups[0][0].shape[0]
    pairs = tuple(len(group) for group in groups)
    frames = [frame for group in groups for frame in group]
    carry = jax.ShapeDtypeStruct((3, rows, LANES), F32)
    held = pltpu.VMEM((len(pairs), keys, 3 * LANES), BF16)
    carried = pltpu.VMEM((3, rows, LANES), F32)
    work = len(pairs) * rows * keys * 3
    return pl.pallas_call(
        functools.partial(attend_kernel, pairs, state is None, last),
        grid_spec=pltpu.PrefetchScalarGridSpec(
            num_scalar_prefetch=1,
            grid=(),
            in_specs=[VMEM] * (1 + len(frames) + (0 if state is None else 2)),
            out_specs=VMEM if last else [VMEM] * 2,
            scratch_shapes=[carried, carried, held] if last else [held],
        ),
        out_shape=jax.ShapeDtypeStruct((rows, 192), BF16) if last else [carry, carry],
        compiler_params=pltpu.CompilerParams(vmem_limit_bytes=40 * 2**20),
        cost_estimate=pl.CostEstimate(
            flops=4 * work * LANES, bytes_accessed=len(frames) * keys * 768, transcendentals=work
        ),
        name="attend",
    )(take, q, *frames, *(() if state is None else state))


def out_kernel(count, core_ref, *refs):
    attn = refs[:count]
    mine = refs[count : 2 * count]
    other = refs[2 * count : 3 * count]
    keep, give = refs[3 * count :]
    rows = keep.shape[0]
    width = mine[0].shape[1]
    core = core_ref[0]
    for weights, side in ((mine, core), (other, 1 - core)):
        total = jnp.dot(attn[0][...], weights[0][...], preferred_element_type=F32)
        for part, weight in zip(attn[1:], weights[1:]):
            total = total + jnp.dot(part[...], weight[...], preferred_element_type=F32)
        span = pl.ds(pl.multiple_of(side * width, LANES), width)
        keep[:, span] = total[:rows]
        give[:, span] = total[rows:].astype(BF16)


def out_project(core, attn, mine, other):
    count = len(attn)
    rows = attn[0].shape[0] // 2
    width = 2 * mine[0].shape[1]
    return pl.pallas_call(
        functools.partial(out_kernel, count),
        grid_spec=pltpu.PrefetchScalarGridSpec(
            num_scalar_prefetch=1, grid=(), in_specs=[VMEM] * (3 * count), out_specs=[VMEM] * 2
        ),
        out_shape=[jax.ShapeDtypeStruct((rows, width), F32), jax.ShapeDtypeStruct((rows, width), BF16)],
        compiler_params=pltpu.CompilerParams(vmem_limit_bytes=32 * 2**20),
        cost_estimate=pl.CostEstimate(
            flops=4 * rows * count * 192 * width, bytes_accessed=count * 192 * width * 2, transcendentals=0
        ),
        name="out_project",
    )(core, *attn, *mine, *other)


def per_device(latents, t_index, window_start, w_mod, w_qkv, q_gain, k_gain, w_out):
    width = latents.shape[2]
    head = q_gain.shape[0]
    own = latents[0]
    frame = lax.axis_index("queue")
    core = frame % 2

    emb = time_features(t_index.astype(F32), w_mod.shape[0])
    active = jax.nn.silu(emb).astype(BF16)
    mod = gather_modulation(jnp.dot(active, w_mod, preferred_element_type=F32))
    shift, scale, gate = mod[:, :width], mod[:, width : 2 * width], mod[:, 2 * width :]

    def columns(which, number):
        at = (3 * number + which) * head
        return w_qkv[:, at : at + head]

    weight = jnp.concatenate(
        [
            columns(0, 0), columns(0, 1), columns(0, 2), jnp.zeros((width, head), BF16),
            columns(1, 0), columns(1, 1), columns(1, 2), columns(2, 1), columns(2, 0), columns(2, 2),
        ],
        axis=1,
    )
    q_row = jnp.concatenate([q_gain, q_gain])[None] * (LOG2E / math.sqrt(head))
    k_row = jnp.concatenate([k_gain, k_gain])[None]
    norms = (shift, scale, weight, q_row, k_row)

    def piece(value, move):
        return send(value, move)

    up1, down1, opp0 = piece(own, along(-1)), piece(own, along(1)), piece(own, across)
    up1, down1, opp0 = lax.optimization_barrier((up1, down1, opp0))
    up2, down2, opp_up1 = piece(up1, along(-1)), piece(down1, along(1)), piece(up1, across)
    up2, down2, opp_up1 = lax.optimization_barrier((up2, down2, opp_up1))
    up3, down3, opp_down1 = piece(up2, along(-1)), piece(down2, along(1)), piece(down1, across)
    up3, down3, opp_down1 = lax.optimization_barrier((up3, down3, opp_down1))
    up4, opp_down2, opp_up2 = piece(up3, along(-1)), piece(opp_down1, along(1)), piece(up2, across)
    up4, opp_down2, opp_up2 = lax.optimization_barrier((up4, opp_down2, opp_up2))
    opp_up3, opp_down3, opp4 = piece(opp_up2, along(-1)), piece(opp_down2, along(1)), piece(up4, across)
    rounds = (
        (own, up1, down1, opp0),
        (up2, down2, opp_up1),
        (up3, down3, opp_down1),
        (up4, opp_down2, opp_up2),
        (opp_up3, opp_down3, opp4),
    )
    order = [(0, 0), (0, 1), (0, 7), (1, 0), (0, 2), (0, 6), (1, 1), (0, 3), (0, 5), (1, 7),
             (0, 4), (1, 6), (1, 2), (1, 3), (1, 5), (1, 4)]
    projected = [project(pieces, *norms) for pieces in rounds]
    q = jnp.concatenate([part[0] for part in projected])
    kv = jnp.concatenate([part[1] for part in projected])

    beside = send(kv, sibling)
    back2 = send(kv, ahead(2))
    front2 = send(kv, ahead(-2))
    third = send(kv, far)
    back2_beside = send(back2, sibling)
    front2_beside = send(front2, sibling)

    lowest = window_start[0] - frame

    def unused(offset):
        return jnp.logical_or(offset < lowest, offset > lowest + 3).astype(jnp.int32)

    take_near = unused(jnp.where(core == 0, 1, -1))
    take_two = unused(-2)
    take_last = unused(jnp.where(core == 0, -1, -3))
    state = attend(q, [(kv,)], jnp.zeros((1,), jnp.int32), None, False)
    state = attend(q, [(beside, third), (back2, front2)], jnp.stack([take_near, take_two]), state, False)
    attn = attend(q, [(back2_beside, front2_beside)], take_last[None], state, True)

    half = width // 2
    mine = [lax.dynamic_slice_in_dim(w_out, core * half, half, 1)]
    other = [lax.dynamic_slice_in_dim(w_out, (1 - core) * half, half, 1)]
    first, _ = lax.optimization_barrier((mine[0], opp_up3))
    ups, downs = [first], [first]
    for step in range(4):
        downs.append(send(downs[-1], along(1)))
        if step < 3:
            ups.append(send(ups[-1], along(-1)))
    by_steps = [mine[0], downs[1], downs[2], downs[3], downs[4], ups[3], ups[2], ups[1]]
    mine = by_steps
    other = other + [send(block, sibling) for block in by_steps[1:]]

    tokens = own.shape[0]
    spots = {place: at for at, place in enumerate(order)}
    parts = []
    for step in range(RING):
        near, opposite = spots[(0, step)], spots[(1, step)]
        rows = jnp.concatenate(
            [attn[near * tokens : (near + 1) * tokens], attn[opposite * tokens : (opposite + 1) * tokens]]
        )
        parts.append(send(rows, lambda q, ring, z, step=step: (q + 1, ring, z + step)))
    keep, give = out_project(core.astype(jnp.int32)[None], parts, mine, other)
    got = send(give, across)
    before = send(own, ahead(1))
    before_gate = send(gate, ahead(1))
    total = keep + got.astype(F32)
    return (before.astype(F32) + before_gate * total).astype(BF16)[None]


def solution(mesh):
    return jax.shard_map(
        per_device,
        mesh=mesh,
        in_specs=(
            P("queue", "heads", None),
            P("queue"),
            P("queue"),
            P(None, "heads"),
            P(None, "heads"),
            P(),
            P(),
            P("heads", None),
        ),
        out_specs=P("queue", "heads", None),
        check_vma=False,
    )
```

```python
import functools
import math

import jax
import jax.numpy as jnp
from jax import lax
from jax.experimental import pallas as pl
from jax.experimental.pallas import tpu as pltpu
from jax.sharding import PartitionSpec as P

F32 = jnp.float32
BF16 = jnp.bfloat16
BOTH = ("queue", "heads")
LANES = 128
HALF = 64
RING = 8
QUEUE = 16
VMEM = pl.BlockSpec(memory_space=pltpu.VMEM)
ANY = pl.BlockSpec(memory_space=pl.ANY)
GRANT = 56 * 2**20
LOG2E = 1.4426950408889634
NT = (((1,), (1,)), ((), ()))
PIECE = 64


def every_device():
    for q in range(QUEUE):
        for h in range(2 * RING):
            yield q, h


def route(move):
    pairs = []
    for q, h in every_device():
        to_q, to_ring, to_z = move(q, h // RING, h % RING)
        pairs.append((q * 2 * RING + h, (to_q % QUEUE) * 2 * RING + to_ring * RING + to_z % RING))
    return pairs


def send(value, move):
    return lax.ppermute(value, BOTH, route(move))


def along(step):
    return lambda q, ring, z: (q, ring, z + step)


def across(q, ring, z):
    return q, 1 - ring, z


def sibling(q, ring, z):
    return q ^ 1, ring, z


def ahead(step):
    return lambda q, ring, z: (q + step, ring, z)


def far(q, ring, z):
    return (q + 3 if q % 2 else q - 3), ring, z


def time_features(steps_float, width):
    half = width // 2
    freqs = jnp.exp(-math.log(10000.0) * jnp.arange(half, dtype=F32) / half)
    angles = steps_float[:, None] * freqs[None, :]
    return jnp.concatenate([jnp.cos(angles), jnp.sin(angles)], axis=1)


def doubled(rows, step):
    return jnp.concatenate([rows, send(rows, along(-step))], axis=0)


def in_order(rows, other):
    place = lax.axis_index("heads")
    start = (RING - place % RING) % RING

    def ring(found):
        found = jnp.concatenate([found[at : at + 1] for at in (0, 4, 2, 6, 1, 5, 3, 7)] * 2)
        return lax.dynamic_slice_in_dim(found, start, RING, 0)

    own, opposite = ring(rows), ring(other)
    trio = jnp.concatenate([own, opposite, own])
    return lax.dynamic_slice_in_dim(trio, (place // RING) * RING, 2 * RING, 0).reshape(1, -1)


def qkv_kernel(count, done, *refs):
    far_pieces, far_weight = refs[:count], refs[count]
    shift, scale, gain_qk, gain_kq = refs[count + 1 : count + 5]
    refs, (pieces, weight, arrived) = refs[count + 5 : -3], refs[-3:]
    copies = [
        pltpu.make_async_copy(source, target, arrived.at[at])
        for at, (source, target) in enumerate(
            [(far_pieces[at], pieces.at[at]) for at in range(count)] + [(far_weight, weight)]
        )
    ]
    for copy in copies:
        copy.start()
    if done:
        q_done, kv_done, q_all, kv_all, normed = refs
        q_all[:done, :] = q_done[...]
        kv_all[:done, :] = kv_done[...]
    else:
        q_all, kv_all, normed = refs
    rows = pieces.shape[1]
    q_out, kv_out = (ref.at[done : done + count * rows] for ref in (q_all, kv_all))
    for at in range(count):
        copies[at].wait()
        x = pieces[at].astype(F32)
        center = jnp.mean(x, axis=-1, keepdims=True)
        x = x - center
        spread = jnp.mean(x * x, axis=-1, keepdims=True)
        x = x * lax.rsqrt(spread + 1e-05) * (1.0 + scale[...]) + shift[...]
        normed[at * rows : (at + 1) * rows, :] = x.astype(BF16)
    copies[count].wait()
    y = lax.dot_general(normed[...], weight[...], NT, preferred_element_type=F32)
    low = lax.broadcasted_iota(jnp.int32, (y.shape[0], LANES), 1) < HALF

    def halves(v):
        first = jnp.sum(jnp.where(low, v, 0.0), axis=-1, keepdims=True)
        second = jnp.sum(jnp.where(low, 0.0, v), axis=-1, keepdims=True)
        return jnp.where(low, first, second) * (1.0 / HALF)

    def norm(v, gain):
        v = v - halves(v)
        return v * lax.rsqrt(halves(v * v) + 1e-06) * gain[...]

    q0k0 = norm(y[:, :LANES], gain_qk)
    v0q1 = y[:, LANES : 2 * LANES]
    k1v1 = y[:, 2 * LANES : 3 * LANES]
    q2k2 = norm(y[:, 3 * LANES : 4 * LANES], gain_qk)
    q1 = pltpu.roll(norm(v0q1, gain_kq), HALF, 1)
    q_out[:, :LANES] = jnp.where(low, 0.0, pltpu.roll(q0k0, HALF, 1)).astype(BF16)
    q_out[:, LANES : 2 * LANES] = jnp.where(low, q1, 0.0).astype(BF16)
    q_out[:, 2 * LANES :] = jnp.where(low, 0.0, pltpu.roll(q2k2, HALF, 1)).astype(BF16)
    kv_out[:, :LANES] = jnp.where(low, norm(k1v1, gain_kq), q0k0).astype(BF16)
    kv_out[:, LANES : 2 * LANES] = jnp.where(low, v0q1, q2k2).astype(BF16)
    kv_out[:, 2 * LANES :] = k1v1.astype(BF16)
    kv_out[:, 2 * LANES : 2 * LANES + HALF] = y[:, 4 * LANES :].astype(BF16)


def project(pieces, shift, scale, weight, gain_qk, gain_kq, before=()):
    count = len(pieces)
    rows, width = pieces[0].shape
    tokens = count * rows
    done = before[0].shape[0] if before else 0
    shape = jax.ShapeDtypeStruct((done + tokens, 3 * LANES), BF16)
    return pl.pallas_call(
        functools.partial(qkv_kernel, count, done),
        in_specs=[ANY] * (count + 1) + [VMEM] * (4 + len(before)),
        out_specs=[VMEM] * 2,
        out_shape=[shape, shape],
        scratch_shapes=[
            pltpu.VMEM((tokens, width), BF16),
            pltpu.VMEM((count, rows, width), BF16),
            pltpu.VMEM(weight.shape, BF16),
            pltpu.SemaphoreType.DMA((count + 1,)),
        ],
        compiler_params=pltpu.CompilerParams(vmem_limit_bytes=GRANT),
        cost_estimate=pl.CostEstimate(
            flops=2 * tokens * width * 576, bytes_accessed=tokens * width * 2 + width * 1152, transcendentals=0
        ),
        name="qkv",
    )(*pieces, weight, shift, scale, gain_qk, gain_kq, *before)


def attend_kernel(queries, groups, block, order, rows, last, take, *refs):
    q_parts, refs = refs[:queries], refs[queries:]
    frames, at = [], 0
    for sizes, paired in groups:
        chunks = len(sizes)
        one = refs[at : at + chunks]
        two = refs[at + chunks : at + 2 * chunks] if paired else None
        at += chunks * (2 if paired else 1)
        frames.append((sizes, one, two))
    refs = refs[at:]
    if order is None:
        top_in, sums_in, refs = refs[0], refs[1], refs[2:]
        q = q_parts[0].at[rows[0] : rows[1]]
    else:
        q, refs = refs[0], refs[1:]
    if last:
        outs, refs = refs[:-5], refs[-5:]
    top, sums, held, values, arrived = refs
    copies, row = [], 0
    for number, (sizes, one, two) in enumerate(frames):
        for at, size in enumerate(sizes):
            target, sem = held.at[row : row + size], arrived.at[len(copies)]
            first = pltpu.make_async_copy(one[at], target, sem)
            if two is None:
                first.start()
            else:
                pl.when(take[number] == 0)(first.start)
                pl.when(take[number] != 0)(pltpu.make_async_copy(two[at], target, sem).start)
            copies.append((row, size, first))
            row += size
    if order is None:
        top[...] = top_in[:, rows[0] : rows[1], :]
        sums[...] = sums_in[:, rows[0] : rows[1], :]
    else:
        sources = [part.at[at : at + PIECE] for part in q_parts for at in range(0, part.shape[0], PIECE)]
        for spot, piece in enumerate(order):
            q[spot * PIECE : (spot + 1) * PIECE, :] = sources[piece][...]
        top[...] = jnp.full_like(top, -1e30)
        sums[...] = jnp.zeros_like(sums)

    for row, size, copy in copies:
        copy.wait()
        span = slice(row, row + size)
        low = lax.broadcasted_iota(jnp.int32, (size, LANES), 1) < HALF
        v0k2 = held[span, LANES : 2 * LANES]
        v2v1 = held[span, 2 * LANES :]
        ones = jnp.ones_like(v2v1)
        values[0, span, :] = jnp.where(low, v0k2, ones)
        values[1, span, :] = jnp.where(low, ones, v2v1)
        values[2, span, :] = jnp.where(low, v2v1, ones)

    @pl.loop(0, (rows[1] - rows[0]) // block)
    def _(turn):
        span = pl.ds(pl.multiple_of(turn * block, block), block)
        scores = [
            lax.dot_general(
                q[span, head * LANES : (head + 1) * LANES],
                held[:, head // 2 * LANES : (head // 2 + 1) * LANES],
                NT,
                preferred_element_type=F32,
            )
            for head in range(3)
        ]
        for head, s in enumerate(scores):
            before = top[head, span, :]
            now = jnp.maximum(before, jnp.max(s, axis=1, keepdims=True))
            p = jnp.exp2(s - now[:, :1]).astype(BF16)
            added = jnp.dot(p, values[head], preferred_element_type=F32)
            sums[head, span, :] = sums[head, span, :] * jnp.exp2(before - now) + added
            top[head, span, :] = now

    if last:
        size = outs[0].shape[0]
        small = lax.broadcasted_iota(jnp.int32, (size, LANES), 1) < HALF
        for number, out in enumerate(outs):
            span = slice(number * size, (number + 1) * size)

            def whole(head, span=span):
                both = sums[head, span, :]
                return both / pltpu.roll(both, HALF, 1)

            out[:, :LANES] = jnp.where(small, whole(0), whole(1)).astype(BF16)
            out[:, LANES:] = whole(2)[:, :HALF].astype(BF16)


def attend(q_parts, groups, take, block, order=None, state=None, rows=None, outs=0):
    total = sum(part.shape[0] for part in q_parts)
    rows = rows or (0, total)
    count = rows[1] - rows[0]
    shapes = tuple((tuple(c.shape[0] for c in one), two is not None) for one, two in groups)
    frames = [chunk for one, two in groups for chunk in (*one, *(two or ()))]
    keys = sum(sum(sizes) for sizes, _ in shapes)
    carry = jax.ShapeDtypeStruct((3, count, LANES), F32)
    carried = pltpu.VMEM((3, count, LANES), F32)
    held = [
        pltpu.VMEM((keys, 3 * LANES), BF16),
        pltpu.VMEM((3, keys, LANES), BF16),
        pltpu.SemaphoreType.DMA((sum(len(sizes) for sizes, _ in shapes),)),
    ]
    if outs:
        out_shape = [jax.ShapeDtypeStruct((count // outs, 192), BF16)] * outs
        scratch = [carried, carried, *held]
    else:
        out_shape, scratch = [carry, carry], held
    if state is None:
        out_shape = [jax.ShapeDtypeStruct((total, 3 * LANES), BF16), *out_shape]
    return pl.pallas_call(
        functools.partial(attend_kernel, len(q_parts), shapes, block, order, rows, outs > 0),
        grid_spec=pltpu.PrefetchScalarGridSpec(
            num_scalar_prefetch=1,
            grid=(),
            in_specs=[VMEM] * len(q_parts) + [ANY] * len(frames) + [VMEM] * (0 if state is None else 2),
            out_specs=[VMEM] * len(out_shape),
            scratch_shapes=scratch,
        ),
        out_shape=out_shape,
        compiler_params=pltpu.CompilerParams(vmem_limit_bytes=24 * 2**20),
        cost_estimate=pl.CostEstimate(
            flops=12 * count * keys * LANES, bytes_accessed=keys * 768, transcendentals=3 * count * keys
        ),
        name="attend",
    )(take, *q_parts, *frames, *(() if state is None else state))


def out_kernel(count, place, *refs):
    parts, (mine, other, keep, give) = refs[:count], refs[count:]
    rows = keep.shape[0]
    width = mine.shape[1]
    heads = mine.shape[0] // count
    core, z = place[0], place[1]
    for weight, side in ((mine, core), (other, 1 - core)):
        total = None
        for step, part in enumerate(parts):
            source = lax.rem(z + count - step, count)
            block = weight[pl.ds(pl.multiple_of(source * heads, heads), heads), :]
            product = jnp.dot(part[...], block, preferred_element_type=F32)
            total = product if total is None else total + product
        span = pl.ds(pl.multiple_of(side * width, LANES), width)
        keep[:, span] = total[:rows]
        give[:, span] = total[rows:].astype(BF16)


def out_project(place, parts, mine, other):
    rows, width = PIECE, 2 * mine.shape[1]
    return pl.pallas_call(
        functools.partial(out_kernel, len(parts)),
        grid_spec=pltpu.PrefetchScalarGridSpec(
            num_scalar_prefetch=1, grid=(), in_specs=[VMEM] * (len(parts) + 2), out_specs=[VMEM] * 2
        ),
        out_shape=[jax.ShapeDtypeStruct((rows, width), F32), jax.ShapeDtypeStruct((rows, width), BF16)],
        compiler_params=pltpu.CompilerParams(vmem_limit_bytes=20 * 2**20),
        cost_estimate=pl.CostEstimate(
            flops=4 * rows * mine.size * 2, bytes_accessed=mine.size * 4, transcendentals=0
        ),
        name="out_project",
    )(place, *parts, mine, other)


def between_chips(kv):
    return send(kv, ahead(2)), send(kv, ahead(-2)), send(kv, far)


def after(value, *others):
    return lax.optimization_barrier((value, others))[0]


def per_device(latents, t_index, window_start, w_mod, w_qkv, q_gain, k_gain, w_out):
    width = latents.shape[2]
    head = q_gain.shape[0]
    own = latents[0]
    frame = lax.axis_index("queue")
    core = frame % 2
    z = lax.axis_index("heads") % RING

    lowest = window_start[0] - frame

    def unused(offset):
        return jnp.logical_or(offset < lowest, offset > lowest + 3).astype(jnp.int32)

    take = jnp.stack([unused(jnp.where(core == 0, 1, -1)), unused(-2), unused(jnp.where(core == 0, -1, -3))])

    emb = time_features(t_index.astype(F32), w_mod.shape[0])
    active = jax.nn.silu(emb).astype(BF16)
    rows = jnp.dot(active, w_mod, preferred_element_type=F32)
    up, down = along(-1), along(1)
    u1, d1, o0 = send(own, up), send(own, down), send(own, across)
    rows = doubled(rows, 4)
    u1, d1, o0, rows, take = lax.optimization_barrier((u1, d1, o0, rows, take))
    u2, d2, ou1 = send(u1, up), send(d1, down), send(u1, across)
    rows = doubled(doubled(rows, 2), 1)
    u2, d2, ou1, d1, rows = lax.optimization_barrier((u2, d2, ou1, d1, rows))
    before = send(after(own, rows), ahead(1))
    u3, d3, od1 = send(u2, up), send(d2, down), send(d1, across)
    mod = in_order(rows, send(rows, across))
    u3, d3, od1, u2, mod = lax.optimization_barrier((u3, d3, od1, u2, mod))
    u4, od2, ou2 = send(u3, up), send(od1, down), send(u2, across)

    shift, scale, gate = mod[:, :width], mod[:, width : 2 * width], mod[:, 2 * width :]
    q_row = q_gain[None] * (LOG2E / math.sqrt(head))
    k_row = k_gain[None]
    norms = (shift, scale, w_qkv.T, jnp.concatenate([q_row, k_row], 1), jnp.concatenate([k_row, q_row], 1))
    q_early, kv_early = project([own, o0, u1, d1, ou1, od1, u2, d2, u3, d3], *norms)

    u4, od2, ou2, q_early, kv_early, before = lax.optimization_barrier((u4, od2, ou2, q_early, kv_early, before))
    ou3, od3, o4 = send(ou2, up), send(od2, down), send(u4, across)
    middle = project([ou2, od2, u4], *norms)
    kv_early = after(kv_early, middle)
    back_early, front_early, third_early = between_chips(kv_early)
    beside_early = send(kv_early, sibling)
    q_late, kv_late = project([ou3, od3, o4], *norms, middle)
    back_late, front_late, third_late = between_chips(kv_late)
    beside_late = send(kv_late, sibling)

    pieces = {0: (0, 1), 1: (2, 4), 7: (3, 5), 2: (6, 10), 6: (7, 11), 3: (8, 13), 5: (9, 14), 4: (12, 15)}
    by_steps = (4, 3, 5, 2, 6, 1, 7, 0)
    order = tuple(piece for steps in by_steps for piece in pieces[steps])
    q, *state = attend([q_early, q_late], [((kv_early, kv_late), None)], take, 512, order)
    back_early, front_early, gate = after((back_early, front_early, gate), state)
    back_early_beside, front_early_beside = send(back_early, sibling), send(front_early, sibling)
    before_gate = send(gate, ahead(1))
    state = attend(
        [q], [((beside_early,), (third_early,)), ((back_early,), (front_early,))], take, 256, state=state
    )
    back_late, front_late = after((back_late, front_late), state)
    back_late_beside, front_late_beside = send(back_late, sibling), send(front_late, sibling)
    q, before_gate = lax.optimization_barrier((q, before_gate))
    remaining = [
        ((beside_late,), (third_late,)),
        ((back_late,), (front_late,)),
        ((back_early_beside, back_late_beside), (front_early_beside, front_late_beside)),
    ]
    attn = attend([q], remaining, take, 256, state=state, outs=RING)

    parts = {
        steps: send(part, lambda q, ring, z, steps=steps: (q + 1, ring, z + steps))
        for steps, part in zip(by_steps, attn)
    }
    parts = [parts[steps] for steps in range(RING)]

    half = width // 2
    mine = after(lax.dynamic_slice_in_dim(w_out, core * half, half, 1), (u4, od2, ou2))
    groups = [list(range(RING)), list(range(RING, 2 * RING))]
    mine = lax.all_gather(mine, "heads", axis=0, tiled=True, axis_index_groups=groups)
    other = send(after(mine, attn[-1]), sibling)

    keep, give = out_project(
        jnp.stack([core, z]).astype(jnp.int32), parts, mine, other
    )
    got = send(give, across)
    total = keep + got.astype(F32)
    return (before.astype(F32) + before_gate * total).astype(BF16)[None]


def solution(mesh):
    return jax.shard_map(
        per_device,
        mesh=mesh,
        in_specs=(
            P("queue", "heads", None),
            P("queue"),
            P("queue"),
            P(None, "heads"),
            P(None, "heads"),
            P(),
            P(),
            P("heads", None),
        ),
        out_specs=P("queue", "heads", None),
        check_vma=False,
    )
```

```python
import functools
import math

import jax
import jax.numpy as jnp
from jax import lax
from jax.experimental import pallas as pl
from jax.experimental.pallas import tpu as pltpu
from jax.sharding import PartitionSpec as P

F32 = jnp.float32
BF16 = jnp.bfloat16
BOTH = ("queue", "heads")
LANES = 128
HALF = 64
RING = 8
QUEUE = 16
VMEM = pl.BlockSpec(memory_space=pltpu.VMEM)
ANY = pl.BlockSpec(memory_space=pl.ANY)
GRANT = 56 * 2**20
LOG2E = 1.4426950408889634
NT = (((1,), (1,)), ((), ()))
PIECE = 64


def every_device():
    for q in range(QUEUE):
        for h in range(2 * RING):
            yield q, h


def route(move):
    pairs = []
    for q, h in every_device():
        to_q, to_ring, to_z = move(q, h // RING, h % RING)
        pairs.append((q * 2 * RING + h, (to_q % QUEUE) * 2 * RING + to_ring * RING + to_z % RING))
    return pairs


def send(value, move):
    return lax.ppermute(value, BOTH, route(move))


def along(step):
    return lambda q, ring, z: (q, ring, z + step)


def across(q, ring, z):
    return q, 1 - ring, z


def sibling(q, ring, z):
    return q ^ 1, ring, z


def ahead(step):
    return lambda q, ring, z: (q + step, ring, z)


def far(q, ring, z):
    return (q + 3 if q % 2 else q - 3), ring, z


def time_features(steps_float, width):
    half = width // 2
    freqs = jnp.exp(-math.log(10000.0) * jnp.arange(half, dtype=F32) / half)
    angles = steps_float[:, None] * freqs[None, :]
    return jnp.concatenate([jnp.cos(angles), jnp.sin(angles)], axis=1)


def doubled(rows, step):
    return jnp.concatenate([rows, send(rows, along(-step))], axis=0)


def in_order(rows, other):
    place = lax.axis_index("heads")
    start = (RING - place % RING) % RING

    def ring(found):
        found = jnp.concatenate([found[at : at + 1] for at in (0, 4, 2, 6, 1, 5, 3, 7)] * 2)
        return lax.dynamic_slice_in_dim(found, start, RING, 0)

    own, opposite = ring(rows), ring(other)
    trio = jnp.concatenate([own, opposite, own])
    return lax.dynamic_slice_in_dim(trio, (place // RING) * RING, 2 * RING, 0).reshape(1, -1)


def qkv_kernel(count, done, *refs):
    far_pieces, far_weight = refs[:count], refs[count]
    shift, scale, gain_qk, gain_kq = refs[count + 1 : count + 5]
    refs, (pieces, weight, arrived) = refs[count + 5 : -3], refs[-3:]
    copies = [
        pltpu.make_async_copy(source, target, arrived.at[at])
        for at, (source, target) in enumerate(
            [(far_pieces[at], pieces.at[at]) for at in range(count)] + [(far_weight, weight)]
        )
    ]
    for copy in copies:
        copy.start()
    if done:
        q_done, kv_done, q_all, kv_all, normed = refs
        q_all[:done, :] = q_done[...]
        kv_all[:done, :] = kv_done[...]
    else:
        q_all, kv_all, normed = refs
    rows = pieces.shape[1]
    q_out, kv_out = (ref.at[done : done + count * rows] for ref in (q_all, kv_all))
    for at in range(count):
        copies[at].wait()
        x = pieces[at].astype(F32)
        center = jnp.mean(x, axis=-1, keepdims=True)
        x = x - center
        spread = jnp.mean(x * x, axis=-1, keepdims=True)
        x = x * lax.rsqrt(spread + 1e-05) * (1.0 + scale[...]) + shift[...]
        normed[at * rows : (at + 1) * rows, :] = x.astype(BF16)
    copies[count].wait()
    y = lax.dot_general(normed[...], weight[...], NT, preferred_element_type=F32)
    low = lax.broadcasted_iota(jnp.int32, (y.shape[0], LANES), 1) < HALF

    def halves(v):
        first = jnp.sum(jnp.where(low, v, 0.0), axis=-1, keepdims=True)
        second = jnp.sum(jnp.where(low, 0.0, v), axis=-1, keepdims=True)
        return jnp.where(low, first, second) * (1.0 / HALF)

    def norm(v, gain):
        v = v - halves(v)
        return v * lax.rsqrt(halves(v * v) + 1e-06) * gain[...]

    q0k0 = norm(y[:, :LANES], gain_qk)
    v0q1 = y[:, LANES : 2 * LANES]
    k1v1 = y[:, 2 * LANES : 3 * LANES]
    q2k2 = norm(y[:, 3 * LANES : 4 * LANES], gain_qk)
    q1 = pltpu.roll(norm(v0q1, gain_kq), HALF, 1)
    q_out[:, :LANES] = jnp.where(low, 0.0, pltpu.roll(q0k0, HALF, 1)).astype(BF16)
    q_out[:, LANES : 2 * LANES] = jnp.where(low, q1, 0.0).astype(BF16)
    q_out[:, 2 * LANES :] = jnp.where(low, 0.0, pltpu.roll(q2k2, HALF, 1)).astype(BF16)
    kv_out[:, :LANES] = jnp.where(low, norm(k1v1, gain_kq), q0k0).astype(BF16)
    kv_out[:, LANES : 2 * LANES] = jnp.where(low, v0q1, q2k2).astype(BF16)
    kv_out[:, 2 * LANES :] = k1v1.astype(BF16)
    kv_out[:, 2 * LANES : 2 * LANES + HALF] = y[:, 4 * LANES :].astype(BF16)


def project(pieces, shift, scale, weight, gain_qk, gain_kq, before=()):
    count = len(pieces)
    rows, width = pieces[0].shape
    tokens = count * rows
    done = before[0].shape[0] if before else 0
    shape = jax.ShapeDtypeStruct((done + tokens, 3 * LANES), BF16)
    return pl.pallas_call(
        functools.partial(qkv_kernel, count, done),
        in_specs=[ANY] * (count + 1) + [VMEM] * (4 + len(before)),
        out_specs=[VMEM] * 2,
        out_shape=[shape, shape],
        scratch_shapes=[
            pltpu.VMEM((tokens, width), BF16),
            pltpu.VMEM((count, rows, width), BF16),
            pltpu.VMEM(weight.shape, BF16),
            pltpu.SemaphoreType.DMA((count + 1,)),
        ],
        compiler_params=pltpu.CompilerParams(vmem_limit_bytes=GRANT),
        cost_estimate=pl.CostEstimate(
            flops=14 * 10**6 * (tokens + 200), bytes_accessed=tokens * width * 2 + width * 1152, transcendentals=0
        ),
        name="qkv",
    )(*pieces, weight, shift, scale, gain_qk, gain_kq, *before)


def attend_kernel(queries, groups, block, order, rows, last, take, *refs):
    q_parts, refs = refs[:queries], refs[queries:]
    frames, at = [], 0
    for sizes, paired in groups:
        chunks = len(sizes)
        one = refs[at : at + chunks]
        two = refs[at + chunks : at + 2 * chunks] if paired else None
        at += chunks * (2 if paired else 1)
        frames.append((sizes, one, two))
    refs = refs[at:]
    if order is None:
        top_in, sums_in, refs = refs[0], refs[1], refs[2:]
        q = q_parts[0].at[rows[0] : rows[1]]
    else:
        q, refs = refs[0], refs[1:]
    if last:
        outs, refs = refs[:-5], refs[-5:]
    top, sums, held, values, arrived = refs
    copies, row = [], 0
    for number, (sizes, one, two) in enumerate(frames):
        for at, size in enumerate(sizes):
            target, sem = held.at[row : row + size], arrived.at[len(copies)]
            first = pltpu.make_async_copy(one[at], target, sem)
            if two is None:
                first.start()
            else:
                pl.when(take[number] == 0)(first.start)
                pl.when(take[number] != 0)(pltpu.make_async_copy(two[at], target, sem).start)
            copies.append((row, size, first))
            row += size
    if order is None:
        top[...] = top_in[:, rows[0] : rows[1], :]
        sums[...] = sums_in[:, rows[0] : rows[1], :]
    else:
        sources = [part.at[at : at + PIECE] for part in q_parts for at in range(0, part.shape[0], PIECE)]
        for spot, piece in enumerate(order):
            q[spot * PIECE : (spot + 1) * PIECE, :] = sources[piece][...]
        top[...] = jnp.full_like(top, -1e30)
        sums[...] = jnp.zeros_like(sums)

    for row, size, copy in copies:
        copy.wait()
        span = slice(row, row + size)
        low = lax.broadcasted_iota(jnp.int32, (size, LANES), 1) < HALF
        v0k2 = held[span, LANES : 2 * LANES]
        v2v1 = held[span, 2 * LANES :]
        ones = jnp.ones_like(v2v1)
        values[0, span, :] = jnp.where(low, v0k2, ones)
        values[1, span, :] = jnp.where(low, ones, v2v1)
        values[2, span, :] = jnp.where(low, v2v1, ones)

    @pl.loop(0, (rows[1] - rows[0]) // block)
    def _(turn):
        span = pl.ds(pl.multiple_of(turn * block, block), block)
        scores = [
            lax.dot_general(
                q[span, head * LANES : (head + 1) * LANES],
                held[:, head // 2 * LANES : (head // 2 + 1) * LANES],
                NT,
                preferred_element_type=F32,
            )
            for head in range(3)
        ]
        for head, s in enumerate(scores):
            before = top[head, span, :]
            now = jnp.maximum(before, jnp.max(s, axis=1, keepdims=True))
            p = jnp.exp2(s - now[:, :1]).astype(BF16)
            added = jnp.dot(p, values[head], preferred_element_type=F32)
            sums[head, span, :] = sums[head, span, :] * jnp.exp2(before - now) + added
            top[head, span, :] = now

    if last:
        size = outs[0].shape[0]
        small = lax.broadcasted_iota(jnp.int32, (size, LANES), 1) < HALF
        for number, out in enumerate(outs):
            span = slice(number * size, (number + 1) * size)

            def whole(head, span=span):
                both = sums[head, span, :]
                return both / pltpu.roll(both, HALF, 1)

            out[:, :LANES] = jnp.where(small, whole(0), whole(1)).astype(BF16)
            out[:, LANES:] = whole(2)[:, :HALF].astype(BF16)


def attend(q_parts, groups, take, block, order=None, state=None, rows=None, outs=0):
    total = sum(part.shape[0] for part in q_parts)
    rows = rows or (0, total)
    count = rows[1] - rows[0]
    shapes = tuple((tuple(c.shape[0] for c in one), two is not None) for one, two in groups)
    frames = [chunk for one, two in groups for chunk in (*one, *(two or ()))]
    keys = sum(sum(sizes) for sizes, _ in shapes)
    carry = jax.ShapeDtypeStruct((3, count, LANES), F32)
    carried = pltpu.VMEM((3, count, LANES), F32)
    held = [
        pltpu.VMEM((keys, 3 * LANES), BF16),
        pltpu.VMEM((3, keys, LANES), BF16),
        pltpu.SemaphoreType.DMA((sum(len(sizes) for sizes, _ in shapes),)),
    ]
    if outs:
        out_shape = [jax.ShapeDtypeStruct((count // outs, 192), BF16)] * outs
        scratch = [carried, carried, *held]
    else:
        out_shape, scratch = [carry, carry], held
    if state is None:
        out_shape = [jax.ShapeDtypeStruct((total, 3 * LANES), BF16), *out_shape]
    return pl.pallas_call(
        functools.partial(attend_kernel, len(q_parts), shapes, block, order, rows, outs > 0),
        grid_spec=pltpu.PrefetchScalarGridSpec(
            num_scalar_prefetch=1,
            grid=(),
            in_specs=[VMEM] * len(q_parts) + [ANY] * len(frames) + [VMEM] * (0 if state is None else 2),
            out_specs=[VMEM] * len(out_shape),
            scratch_shapes=scratch,
        ),
        out_shape=out_shape,
        compiler_params=pltpu.CompilerParams(vmem_limit_bytes=24 * 2**20),
        cost_estimate=pl.CostEstimate(
            flops=54 * count * keys * LANES, bytes_accessed=keys * 768, transcendentals=3 * count * keys
        ),
        name="attend",
    )(take, *q_parts, *frames, *(() if state is None else state))


def out_kernel(count, place, *refs):
    parts, (mine, other, keep, give) = refs[:count], refs[count:]
    rows = keep.shape[0]
    width = mine.shape[1]
    heads = mine.shape[0] // count
    core, z = place[0], place[1]
    for weight, side in ((mine, core), (other, 1 - core)):
        total = None
        for step, part in enumerate(parts):
            source = lax.rem(z + count - step, count)
            block = weight[pl.ds(pl.multiple_of(source * heads, heads), heads), :]
            product = jnp.dot(part[...], block, preferred_element_type=F32)
            total = product if total is None else total + product
        span = pl.ds(pl.multiple_of(side * width, LANES), width)
        keep[:, span] = total[:rows]
        give[:, span] = total[rows:].astype(BF16)


def out_project(place, parts, mine, other):
    rows, width = PIECE, 2 * mine.shape[1]
    return pl.pallas_call(
        functools.partial(out_kernel, len(parts)),
        grid_spec=pltpu.PrefetchScalarGridSpec(
            num_scalar_prefetch=1, grid=(), in_specs=[VMEM] * (len(parts) + 2), out_specs=[VMEM] * 2
        ),
        out_shape=[jax.ShapeDtypeStruct((rows, width), F32), jax.ShapeDtypeStruct((rows, width), BF16)],
        compiler_params=pltpu.CompilerParams(vmem_limit_bytes=20 * 2**20),
        cost_estimate=pl.CostEstimate(
            flops=4 * rows * mine.size * 2, bytes_accessed=mine.size * 4, transcendentals=0
        ),
        name="out_project",
    )(place, *parts, mine, other)


def between_chips(kv):
    return send(kv, ahead(2)), send(kv, ahead(-2)), send(kv, far)


def after(value, *others):
    return lax.optimization_barrier((value, others))[0]


def per_device(latents, t_index, window_start, w_mod, w_qkv, q_gain, k_gain, w_out):
    width = latents.shape[2]
    head = q_gain.shape[0]
    own = latents[0]
    frame = lax.axis_index("queue")
    core = frame % 2
    z = lax.axis_index("heads") % RING

    lowest = window_start[0] - frame

    def unused(offset):
        return jnp.logical_or(offset < lowest, offset > lowest + 3).astype(jnp.int32)

    take = jnp.stack([unused(jnp.where(core == 0, 1, -1)), unused(-2), unused(jnp.where(core == 0, -1, -3))])

    emb = time_features(t_index.astype(F32), w_mod.shape[0])
    active = jax.nn.silu(emb).astype(BF16)
    rows = jnp.dot(active, w_mod, preferred_element_type=F32)
    up, down = along(-1), along(1)
    u1, d1, o0 = send(own, up), send(own, down), send(own, across)
    rows = doubled(rows, 4)
    u1, d1, o0, rows, take = lax.optimization_barrier((u1, d1, o0, rows, take))
    u2, d2, ou1 = send(u1, up), send(d1, down), send(u1, across)
    rows = doubled(doubled(rows, 2), 1)
    u2, d2, ou1, d1, rows = lax.optimization_barrier((u2, d2, ou1, d1, rows))
    before = send(after(own, rows), ahead(1))
    u3, d3, od1 = send(u2, up), send(d2, down), send(d1, across)
    mod = in_order(rows, send(rows, across))
    u3, d3, od1, u2, mod = lax.optimization_barrier((u3, d3, od1, u2, mod))
    u4, od2, ou2 = send(u3, up), send(od1, down), send(u2, across)

    shift, scale, gate = mod[:, :width], mod[:, width : 2 * width], mod[:, 2 * width :]
    q_row = q_gain[None] * (LOG2E / math.sqrt(head))
    k_row = k_gain[None]
    norms = (shift, scale, w_qkv.T, jnp.concatenate([q_row, k_row], 1), jnp.concatenate([k_row, q_row], 1))
    q_early, kv_early = project([own, o0, u1, d1, ou1, od1, u2, d2, u3, d3], *norms)

    u4, od2, ou2, q_early, kv_early, before = lax.optimization_barrier((u4, od2, ou2, q_early, kv_early, before))
    ou3, od3, o4 = send(ou2, up), send(od2, down), send(u4, across)
    middle = project([ou2, od2, u4], *norms)
    kv_early = after(kv_early, middle)
    back_early, front_early, third_early = between_chips(kv_early)
    beside_early = send(kv_early, sibling)
    q_late, kv_late = project([ou3, od3, o4], *norms, middle)
    back_late, front_late, third_late = between_chips(kv_late)
    beside_late = send(kv_late, sibling)

    pieces = {0: (0, 1), 1: (2, 4), 7: (3, 5), 2: (6, 10), 6: (7, 11), 3: (8, 13), 5: (9, 14), 4: (12, 15)}
    by_steps = (4, 3, 5, 2, 6, 1, 7, 0)
    order = tuple(piece for steps in by_steps for piece in pieces[steps])
    q, *state = attend([q_early, q_late], [((kv_early, kv_late), None)], take, 512, order)
    back_early, front_early, gate = after((back_early, front_early, gate), state)
    back_early_beside, front_early_beside = send(back_early, sibling), send(front_early, sibling)
    before_gate = send(gate, ahead(1))
    near_early = [
        ((beside_early,), (third_early,)),
        ((back_early,), (front_early,)),
        ((back_early_beside,), (front_early_beside,)),
    ]
    state = attend([q], near_early, take, 256, state=state)
    back_late, front_late = after((back_late, front_late), state)
    back_late_beside, front_late_beside = send(back_late, sibling), send(front_late, sibling)
    q, before_gate = lax.optimization_barrier((q, before_gate))
    remaining = [
        ((beside_late,), (third_late,)),
        ((back_late,), (front_late,)),
        ((back_late_beside,), (front_late_beside,)),
    ]
    attn = attend([q], remaining, take, 256, state=state, outs=RING)

    parts = {
        steps: send(part, lambda q, ring, z, steps=steps: (q + 1, ring, z + steps))
        for steps, part in zip(by_steps, attn)
    }
    parts = [parts[steps] for steps in range(RING)]

    half = width // 2
    mine = after(lax.dynamic_slice_in_dim(w_out, core * half, half, 1), (u4, od2, ou2))
    groups = [list(range(RING)), list(range(RING, 2 * RING))]
    mine = lax.all_gather(mine, "heads", axis=0, tiled=True, axis_index_groups=groups)
    other = send(after(mine, attn[-1]), sibling)

    keep, give = out_project(
        jnp.stack([core, z]).astype(jnp.int32), parts, mine, other
    )
    got = send(give, across)
    total = keep + got.astype(F32)
    return (before.astype(F32) + before_gate * total).astype(BF16)[None]


def solution(mesh):
    return jax.shard_map(
        per_device,
        mesh=mesh,
        in_specs=(
            P("queue", "heads", None),
            P("queue"),
            P("queue"),
            P(None, "heads"),
            P(None, "heads"),
            P(),
            P(),
            P("heads", None),
        ),
        out_specs=P("queue", "heads", None),
        check_vma=False,
    )
```
